512 devices in a mesh: pb: 16 (over y, core), ha: 32 (over z, x).
Axes of the slice: x: 4, y: 8, z: 8, core: 2. Of those that a mesh axis runs over, the one named last changes fastest.
Arguments:
- query_embed: bfloat16 [16384, 128], P(('pb', 'ha')), may hold values from -6 to 6
- host_embed: bfloat16 [65536, 128], P(('pb', 'ha')), may hold values from -6 to 6
- query_degree: int32 [16384], P(('pb', 'ha')), may hold values from 8 to 128
- host_degree: int32 [65536], P(('pb', 'ha')), may hold values from 8 to 128
- tile_rows: int32 [8192], P(('pb', 'ha')), may hold values from 0 to 127, as said below
- tile_cols: int32 [8192], P(('pb', 'ha')), may hold values from 0 to 511, as said below
- tile_counts: int32 [8192, 128, 128], P(('pb', 'ha')), may hold values from 0 to 3, as said below
- keep_mask: int32 [2, 8192], P(None, ('pb', 'ha')), may hold values 0 or 1
- live_tiles: int32 [512], P(('pb', 'ha')), may hold values from 4 to 16, as said below
Outputs:
- query_out: bfloat16 [2, 16384, 128], P(None, ('pb', 'ha'))
- host_out: bfloat16 [2, 65536, 128], P(None, ('pb', 'ha'))
The draws below stay inside these ranges and needn't reach their ends.
Inputs may be any that keep to these rules, and one draw needn't show every extreme that they name: `tile_rows`: slot s of group d = s // 16 names a query block in [p * 8, (p + 1) * 8) with p = d // 32, for live and stale slots alike. `tile_cols`: slot s of group d = s // 16 names a host block c with c % 32 == d % 32, for live and stale slots alike. `tile_counts`: stale slots (at or past their group's live count) hold arbitrary counts. `live_tiles`: in every draw some slot group has all 16 slots live.
All inputs are finite; a program needn't handle non-finite values. No bound on the sum of `keep_mask` on one device may be relied on, other than what follows from the above.
Results may differ from the reference program's by a relative error of at most 0.02.
Values may be sent and summed in bfloat16 or wider, within the bound.
No kernel may reach another device: no remote copies, remote signals or barrier semaphores. Data moves between devices by JAX's collectives and lax.ppermute only.
A program may use at most 64 MiB of HBM per device.

```python
import jax
import jax.numpy as jnp
from jax import lax

DIM = 128
BLOCK = 128
QDEV = 32
CAP = 16
LAYERS = 2
QUERIES = 16384
HOSTS = 65536
QBLK = 8
TILES = 8192
N_PB = 16
N_HA = 32
DEVICES = 512


def draw_tile_rows(key, part):
    key = jax.random.fold_in(key, 11)
    slot_ids = jnp.arange(TILES, dtype=jnp.int32)
    slab_index = slot_ids // CAP // N_HA
    offset = jax.random.randint(key, (TILES,), 0, QBLK)
    return (slab_index * QBLK + offset).astype(jnp.int32)


def draw_tile_cols(key, part):
    key = jax.random.fold_in(key, 12)
    slot_ids = jnp.arange(TILES, dtype=jnp.int32)
    host_column = slot_ids // CAP % N_HA
    within = jax.random.randint(key, (TILES,), 0, N_PB)
    return (host_column + N_HA * within).astype(jnp.int32)


def draw_tile_counts(key, part):
    key = jax.random.fold_in(key, 13)
    return jax.random.randint(key, (TILES, BLOCK, BLOCK), 0, 4).astype(jnp.int32)


def draw_live_tiles(key, part):
    key = jax.random.fold_in(key, 14)
    first_key, second_key = jax.random.split(key)
    live_count = jax.random.randint(first_key, (DEVICES,), CAP // 4, CAP + 1)
    full_group = jax.random.randint(second_key, (), 0, DEVICES)
    return live_count.at[full_group].set(CAP).astype(jnp.int32)


def touch_ends(array, rng, smallest, high):
    longest = array.shape.index(max(array.shape))
    spots = []
    for shift in (0, 1):
        where = [jax.random.randint(jax.random.fold_in(rng, axis), (), 0, length) for axis, length in enumerate(array.shape)]
        where[longest] = (where[longest] + shift) % array.shape[longest]
        spots.append(tuple(where))
    return array.at[spots[0]].set(smallest).at[spots[1]].set(high)


def levels(own_key, shape, pieces, least, top_value):
    level = 1.0
    for dim, parts in pieces:
        steps = jax.random.uniform(jax.random.fold_in(jax.random.fold_in(own_key, 6), dim), (parts,), jnp.float32, least / len(pieces), top_value / len(pieces))
        level = level * jnp.repeat(jnp.exp(steps), shape[dim] // parts).reshape((-1,) + (1,) * (len(shape) - 1 - dim))
    return level


def centred(rng, shape, spread, most, shards=(), kind=jnp.bfloat16):
    drawn = spread * jax.random.normal(rng, shape, jnp.float32)
    if shards:
        drawn = drawn * levels(rng, shape, shards, -0.22, 0.18)
    return jnp.clip(drawn, -most, most).astype(kind)


def setup_inputs(seed: int = 0) -> dict:
    arg_keys = jax.random.split(jax.random.key(seed), 10)
    query_embed = centred(arg_keys[0], (QUERIES, DIM), 1.0, 6.0, ((0, 512),))
    host_embed = centred(arg_keys[1], (HOSTS, DIM), 1.0, 6.0, ((0, 512),))
    query_degree = touch_ends(jax.random.randint(arg_keys[2], (QUERIES,), 8, 129), jax.random.fold_in(arg_keys[2], 1), 8, 128).astype(jnp.int32)
    host_degree = touch_ends(jax.random.randint(arg_keys[3], (HOSTS,), 8, 129), jax.random.fold_in(arg_keys[3], 1), 8, 128).astype(jnp.int32)
    tile_rows = draw_tile_rows(jax.random.fold_in(arg_keys[9], 71), 0)
    tile_cols = draw_tile_cols(jax.random.fold_in(arg_keys[9], 71), 0)
    tile_counts = draw_tile_counts(jax.random.fold_in(arg_keys[9], 71), 0)
    keep_mask = touch_ends((jax.random.randint(arg_keys[7], (2, TILES), 0, 5) < 4).astype(jnp.int32), jax.random.fold_in(arg_keys[7], 1), 0, 1)
    live_tiles = draw_live_tiles(jax.random.fold_in(arg_keys[9], 71), 0)
    return dict(query_embed=query_embed, host_embed=host_embed, query_degree=query_degree, host_degree=host_degree, tile_rows=tile_rows, tile_cols=tile_cols, tile_counts=tile_counts, keep_mask=keep_mask, live_tiles=live_tiles)


def reference(query_embed, host_embed, query_degree, host_degree, tile_rows, tile_cols, tile_counts, keep_mask, live_tiles):
    embed_width = query_embed.shape[1]
    slab_rows = QDEV * N_HA
    scale_query = lax.rsqrt(query_degree.astype(jnp.float32))[:, None]
    scale_host = lax.rsqrt(host_degree.astype(jnp.float32))[:, None]
    slot_ids = jnp.arange(CAP, dtype=jnp.int32)

    def propagate(query_now, host_now):
        sent_query = (scale_query * query_now.astype(jnp.float32)).astype(jnp.bfloat16)
        sent_host = (scale_host * host_now.astype(jnp.float32)).astype(jnp.bfloat16)
        query_blocks = sent_query.reshape(2, QUERIES // BLOCK, BLOCK, embed_width)
        host_blocks = sent_host.reshape(2, DEVICES, BLOCK, embed_width)

        def one_group(group_index, totals):
            query_sum, host_sum = totals
            slab_index = group_index // N_HA
            host_column = group_index % N_HA
            first_slot = (group_index * CAP).astype(jnp.int32)
            counts = lax.dynamic_slice_in_dim(tile_counts, first_slot, CAP, 0)
            keep_part = lax.dynamic_slice_in_dim(keep_mask, first_slot, CAP, 1)
            group_rows = lax.dynamic_slice_in_dim(tile_rows, first_slot, CAP, 0)
            group_cols = lax.dynamic_slice_in_dim(tile_cols, first_slot, CAP, 0)
            slot_live = (slot_ids < live_tiles[group_index]).astype(jnp.int32)
            weight = (counts[None] * (keep_part * slot_live[None])[:, :, None, None]).astype(jnp.float32)
            host_rows = jnp.take(host_blocks, group_cols, axis=1).astype(jnp.float32)
            query_rows = jnp.take(query_blocks, group_rows, axis=1).astype(jnp.float32)
            query_prod = jnp.einsum('vtqh,vthw->vtqw', weight, host_rows)
            host_prod = jnp.einsum('vtqh,vtqw->vthw', weight, query_rows)
            local_rows = group_rows - slab_index * QBLK
            local_cols = group_cols // N_HA
            row_hot = (jnp.arange(QBLK, dtype=jnp.int32)[:, None] == local_rows[None, :]).astype(jnp.float32)
            col_hot = (jnp.arange(N_PB, dtype=jnp.int32)[:, None] == local_cols[None, :]).astype(jnp.float32)
            query_part = jnp.einsum('bt,vtqw->vbqw', row_hot, query_prod, precision=lax.Precision.HIGHEST).astype(jnp.bfloat16)
            host_part = jnp.einsum('bt,vthw->vbhw', col_hot, host_prod, precision=lax.Precision.HIGHEST).astype(jnp.bfloat16)
            query_part = lax.optimization_barrier(query_part)
            host_part = lax.optimization_barrier(host_part)
            query_sum = query_sum.at[:, slab_index].add(query_part.reshape(2, slab_rows, embed_width).astype(jnp.float32))
            host_sum = host_sum.at[:, :, host_column].add(host_part.astype(jnp.float32))
            return (query_sum, host_sum)
        zeros_query = jnp.zeros((2, N_PB, slab_rows, embed_width), jnp.float32)
        zeros_host = jnp.zeros((2, N_PB, N_HA, BLOCK, embed_width), jnp.float32)
        query_sum, host_sum = lax.fori_loop(0, DEVICES, one_group, (zeros_query, zeros_host))
        query_next = (scale_query * query_sum.reshape(2, QUERIES, embed_width)).astype(jnp.bfloat16)
        host_next = (scale_host * host_sum.reshape(2, HOSTS, embed_width)).astype(jnp.bfloat16)
        return (query_next, host_next)
    query_now = jnp.stack([query_embed, query_embed])
    host_now = jnp.stack([host_embed, host_embed])
    query_total = query_now.astype(jnp.float32)
    host_total = host_now.astype(jnp.float32)
    for layer_index in range(LAYERS):
        query_now, host_now = propagate(query_now, host_now)
        query_total = query_total + query_now.astype(jnp.float32)
        host_total = host_total + host_now.astype(jnp.float32)
    query_out = (query_total / (LAYERS + 1)).astype(jnp.bfloat16)
    host_out = (host_total / (LAYERS + 1)).astype(jnp.bfloat16)
    return (query_out, host_out)
```

```python
import functools

import jax
import jax.numpy as jnp
from jax import lax
from jax.experimental import pallas as pl
from jax.experimental.pallas import tpu as pltpu
from jax.sharding import PartitionSpec as P

DIM = 128
BLOCK = 128
CAP = 16
LAYERS = 2
BOTH = 2 * DIM

SMEM = pl.BlockSpec(memory_space=pltpu.SMEM)
VMEM = pl.BlockSpec(memory_space=pltpu.VMEM)


def add_views(acc_ref, slot, keep_ref, s, prod):
    first = prod[:, :DIM]
    second = prod[:, -DIM:]
    acc_ref[slot, :, :DIM] += keep_ref[0, s] * first
    acc_ref[slot, :, DIM:] += keep_ref[1, s] * second


def host_kernel(
    rows_ref, slots_ref, keep_ref, w_ref, q_ref, own_ref, send_ref, acc_ref
):
    acc_ref[...] = jnp.zeros_like(acc_ref)
    for s in range(CAP):
        at = pl.multiple_of(rows_ref[s] * BLOCK, BLOCK)
        prod = lax.dot_general(
            w_ref[s],
            q_ref[pl.ds(at, BLOCK), :],
            (((0,), (0,)), ((), ())),
            preferred_element_type=jnp.float32,
        )
        add_views(acc_ref, slots_ref[s], keep_ref, s, prod)
    half = acc_ref.shape[0] // 2
    own_ref[...] = acc_ref[:half]
    send_ref[...] = acc_ref[half:].astype(jnp.bfloat16)


def pick(pieces, slot, width):
    size = pieces[0].shape[0] // BLOCK
    at = pl.multiple_of((slot % size) * BLOCK, BLOCK)
    block = pieces[0][pl.ds(at, BLOCK), :width]
    if len(pieces) == 2:
        block = jnp.where(slot < size, block, pieces[1][pl.ds(at, BLOCK), :width])
    return block


def query_kernel(
    rows_ref, cols_ref, keep_ref, w_ref, *refs, width
):
    *pieces, part_ref, acc_ref = refs
    acc_ref[...] = jnp.zeros_like(acc_ref)
    for s in range(CAP):
        host = pick(pieces, cols_ref[s], width)
        prod = jnp.dot(w_ref[s], host, preferred_element_type=jnp.float32)
        add_views(acc_ref, rows_ref[s], keep_ref, s, prod)
    part_ref[...] = acc_ref[...].astype(jnp.bfloat16)


def cost(width):
    return pl.CostEstimate(
        flops=2 * CAP * BLOCK * BLOCK * width, bytes_accessed=3 * 2**20, transcendentals=0
    )


def host_sums(rows, slots, keep, weights, slab, blocks):
    half = blocks // 2
    return pl.pallas_call(
        host_kernel,
        out_shape=(
            jax.ShapeDtypeStruct((half, BLOCK, BOTH), jnp.float32),
            jax.ShapeDtypeStruct((half, BLOCK, BOTH), jnp.bfloat16),
        ),
        in_specs=[SMEM, SMEM, SMEM, VMEM, VMEM],
        out_specs=(VMEM, VMEM),
        scratch_shapes=[pltpu.VMEM((blocks, BLOCK, BOTH), jnp.float32)],
        cost_estimate=cost(slab.shape[1]),
        compiler_params=pltpu.CompilerParams(vmem_limit_bytes=24 * 2**20),
        name="host_sums",
    )(rows, slots, keep, weights, slab)


def query_sums(rows, cols, keep, weights, pieces, blocks, width):
    return pl.pallas_call(
        functools.partial(query_kernel, width=width),
        out_shape=jax.ShapeDtypeStruct((blocks, BLOCK, BOTH), jnp.bfloat16),
        in_specs=[SMEM, SMEM, SMEM] + [VMEM] * (1 + len(pieces)),
        out_specs=VMEM,
        scratch_shapes=[pltpu.VMEM((blocks, BLOCK, BOTH), jnp.float32)],
        cost_estimate=cost(width),
        compiler_params=pltpu.CompilerParams(vmem_limit_bytes=24 * 2**20),
        name="query_sums",
    )(rows, cols, keep, weights, *pieces)


def exchange(blocks, axis, groups=None):
    return lax.all_to_all(blocks, axis, 0, 0, axis_index_groups=groups, tiled=True)


def spread(local, axis):
    size = lax.axis_size(axis)
    copies = jnp.broadcast_to(local[None], (size,) + local.shape)
    return exchange(copies, axis).reshape(size * local.shape[0], local.shape[1])


def split_views(both):
    return jnp.stack([both[:, :DIM], both[:, DIM:]])


def per_device(
    query_embed,
    host_embed,
    query_degree,
    host_degree,
    tile_rows,
    tile_cols,
    tile_counts,
    keep_mask,
    live_tiles,
):
    n_pb, n_ha = lax.axis_size("pb"), lax.axis_size("ha")
    query_local = query_embed.shape[0]
    slab_blocks = n_ha * query_local // BLOCK
    chips = n_pb // 2
    core = lax.axis_index("pb") % 2
    same_core = [[2 * y + c for y in range(chips)] for c in range(2)]
    other_core = [(i, i ^ 1) for i in range(n_pb)]

    rows = tile_rows % slab_blocks
    cols = tile_cols // n_ha
    slots = ((cols % 2) ^ core) * chips + cols // 2
    live = jnp.arange(CAP, dtype=jnp.int32) < live_tiles[0]
    keep = (keep_mask * live[None]).astype(jnp.float32)
    weights = tile_counts.astype(jnp.bfloat16)
    scale_query = lax.rsqrt(query_degree.astype(jnp.float32))[:, None]
    scale_host = lax.rsqrt(host_degree.astype(jnp.float32))[:, None]

    def sent(scale, now):
        return (scale * now.astype(jnp.float32)).astype(jnp.bfloat16)

    def reduce_query(part):
        pieces = exchange(part.reshape(n_ha, query_local, BOTH), "ha")
        return sent(scale_query, jnp.sum(pieces.astype(jnp.float32), axis=0))

    def pair_host(own, send):
        other = lax.ppermute(send, "pb", other_core)
        return (own + other.astype(jnp.float32)).astype(jnp.bfloat16)

    def reduce_host(pair):
        pieces = exchange(pair, "pb", same_core)
        return sent(scale_host, jnp.sum(pieces.astype(jnp.float32), axis=0))

    def gather_host(local):
        copies = jnp.broadcast_to(local[None], (chips,) + local.shape)
        mine = exchange(copies, "pb", same_core).reshape(chips * BLOCK, local.shape[1])
        return mine, lax.ppermute(mine, "pb", other_core)

    slab = spread(sent(scale_query, query_embed), "ha")
    pieces = gather_host(sent(scale_host, host_embed))
    own, send = host_sums(rows, slots, keep, weights, slab, n_pb)
    pair = pair_host(own, send)
    host_1 = reduce_host(pair)
    sent_host = sent(scale_host, host_1)
    part = query_sums(rows, slots, keep, weights, pieces, slab_blocks, DIM)
    query_1 = reduce_query(part)

    pieces = gather_host(sent_host)
    slab = spread(sent(scale_query, query_1), "ha")
    own, send = host_sums(rows, slots, keep, weights, slab, n_pb)
    pair = pair_host(own, send)
    host_2 = reduce_host(pair)
    part = query_sums(rows, slots, keep, weights, pieces, slab_blocks, BOTH)
    query_2 = reduce_query(part)

    def mean(embed, one, two):
        zero = embed.astype(jnp.float32)[None]
        total = zero + split_views(one).astype(jnp.float32) + split_views(two).astype(jnp.float32)
        return (total / (LAYERS + 1)).astype(jnp.bfloat16)

    return (mean(query_embed, query_1, query_2), mean(host_embed, host_1, host_2))


def solution(mesh):
    in_specs = (
        P(("pb", "ha"), None),
        P(("pb", "ha"), None),
        P(("pb", "ha")),
        P(("pb", "ha")),
        P(("pb", "ha")),
        P(("pb", "ha")),
        P(("pb", "ha"), None, None),
        P(None, ("pb", "ha")),
        P(("pb", "ha")),
    )
    out_specs = (P(None, ("pb", "ha"), None), P(None, ("pb", "ha"), None))
    return jax.shard_map(
        per_device, mesh=mesh, in_specs=in_specs, out_specs=out_specs, check_vma=False
    )
```

```python
import functools

import jax
import jax.numpy as jnp
from jax import lax
from jax.experimental import pallas as pl
from jax.experimental.pallas import tpu as pltpu
from jax.sharding import PartitionSpec as P

DIM = 128
BLOCK = 128
CAP = 16
LAYERS = 2
BOTH = 2 * DIM

SMEM = pl.BlockSpec(memory_space=pltpu.SMEM)
VMEM = pl.BlockSpec(memory_space=pltpu.VMEM)


def call(kernel, name, outs, ins, scratch=(), flops=0):
    return pl.pallas_call(
        kernel,
        out_shape=outs,
        in_specs=ins,
        out_specs=jax.tree.map(lambda _: VMEM, outs),
        scratch_shapes=scratch,
        cost_estimate=pl.CostEstimate(flops=flops, bytes_accessed=2**21, transcendentals=0),
        compiler_params=pltpu.CompilerParams(vmem_limit_bytes=24 * 2**20),
        name=name,
    )


def half(*shape):
    return jax.ShapeDtypeStruct(shape, jnp.bfloat16)


def single(*shape):
    return jax.ShapeDtypeStruct(shape, jnp.float32)


def add_views(acc_ref, block, keep_ref, s, prod):
    acc_ref[block, :, :DIM] += keep_ref[0, s] * prod[:, :DIM]
    acc_ref[block, :, DIM:] += keep_ref[1, s] * prod[:, -DIM:]


def host_kernel(
    rows_ref, slots_ref, keep_ref, w_ref, q_ref, own_ref, send_ref, acc_ref, *, lanes
):
    acc_ref[...] = jnp.zeros_like(acc_ref)
    owned = own_ref.shape[0]
    n = BLOCK // q_ref.shape[1]
    for s in range(CAP):
        q = q_ref[pl.ds(rows_ref[s] * n, n), :, -lanes:].reshape(BLOCK, lanes)
        prod = lax.dot_general(
            w_ref[s], q, (((0,), (0,)), ((), ())), preferred_element_type=jnp.float32
        )
        add_views(acc_ref, slots_ref[s], keep_ref, s, prod)
    own_ref[...] = acc_ref[:owned]
    send_ref[...] = acc_ref[owned:].astype(jnp.bfloat16)


def query_kernel(rows_ref, slots_ref, keep_ref, w_ref, mine_ref, other_ref, *refs):
    *extra, out_ref, acc_ref = refs
    acc_ref[...] = jnp.zeros_like(acc_ref)
    owned = mine_ref.shape[0]
    for s in range(CAP):
        slot = slots_ref[s]
        at = slot % owned
        host = jnp.where(slot < owned, mine_ref[at, :BLOCK], other_ref[at])
        prod = jnp.dot(w_ref[s], host, preferred_element_type=jnp.float32)
        add_views(acc_ref, rows_ref[s], keep_ref, s, prod)
    shape = out_ref.shape[:2]
    out_ref[:, :, :BOTH] = acc_ref[...].astype(jnp.bfloat16).reshape(shape + (BOTH,))
    if extra:
        out_ref[:, :, BOTH:] = jnp.broadcast_to(extra[0][...][None], shape + (DIM,))


def next_rows(scale_ref, total):
    now = (scale_ref[...] * total).astype(jnp.bfloat16)
    return now, (scale_ref[...] * now.astype(jnp.float32)).astype(jnp.bfloat16)


def query_update_kernel(in_ref, scale_ref, now_ref, copies_ref):
    total = jnp.sum(in_ref[:, :, :BOTH].astype(jnp.float32), axis=0)
    now, sent = next_rows(scale_ref, total)
    now_ref[...] = now
    copies_ref[...] = jnp.broadcast_to(sent[None], copies_ref.shape)


def host_update_kernel(in_ref, scale_ref, own_ref, other_ref, now_ref, out_ref):
    now, sent = next_rows(scale_ref, jnp.sum(in_ref[...].astype(jnp.float32), axis=0))
    now_ref[...] = now
    out_ref[:, :BLOCK] = jnp.broadcast_to(sent[None], in_ref.shape)
    pair = own_ref[...] + other_ref[...].astype(jnp.float32)
    out_ref[:, BLOCK:] = pair.astype(jnp.bfloat16)


def exchange(blocks, axis, groups=None):
    return lax.all_to_all(blocks, axis, 0, 0, axis_index_groups=groups, tiled=True)


def split_views(both):
    return jnp.stack([both[:, :DIM], both[:, DIM:]])


def per_device(
    query_embed,
    host_embed,
    query_degree,
    host_degree,
    tile_rows,
    tile_cols,
    tile_counts,
    keep_mask,
    live_tiles,
):
    n_pb, n_ha = lax.axis_size("pb"), lax.axis_size("ha")
    local = query_embed.shape[0]
    slab_blocks = n_ha * local // BLOCK
    chips = n_pb // 2
    core = lax.axis_index("pb") % 2
    same_core = [[2 * y + c for y in range(chips)] for c in range(2)]

    rows = tile_rows % slab_blocks
    cols = tile_cols // n_ha
    slots = ((cols % 2) ^ core) * chips + cols // 2
    live = jnp.arange(CAP, dtype=jnp.int32) < live_tiles[0]
    keep = (keep_mask * live[None]).astype(jnp.float32)
    weights = tile_counts.astype(jnp.bfloat16)
    scale_query = lax.rsqrt(query_degree.astype(jnp.float32))[:, None]
    scale_host = lax.rsqrt(host_degree.astype(jnp.float32))[:, None]

    def sent(scale, now):
        return (scale * now.astype(jnp.float32)).astype(jnp.bfloat16)

    def swap_core(blocks):
        return lax.ppermute(blocks, "pb", [(i, i ^ 1) for i in range(n_pb)])

    def host_sums(slab, lanes, blocks):
        return call(
            functools.partial(host_kernel, lanes=lanes),
            "host_sums",
            (single(chips, BLOCK, BOTH), half(chips, BLOCK, BOTH)),
            [SMEM, SMEM, SMEM, VMEM, VMEM],
            [pltpu.VMEM((n_pb, BLOCK, BOTH), jnp.float32)],
            2 * CAP * BLOCK * BLOCK * lanes,
        )(rows, blocks, keep, weights, slab)

    def query_sums(mine, other, *extra):
        lanes = mine.shape[2]
        return call(
            query_kernel,
            "query_sums",
            half(n_ha, local, BOTH + DIM * len(extra)),
            [SMEM, SMEM, SMEM] + [VMEM] * (3 + len(extra)),
            [pltpu.VMEM((slab_blocks, BLOCK, BOTH), jnp.float32)],
            2 * CAP * BLOCK * BLOCK * lanes,
        )(rows, slots, keep, weights, mine, other, *extra)

    sent_host = sent(scale_host, host_embed)
    mine = exchange(jnp.broadcast_to(sent_host[None], (chips, BLOCK, DIM)), "pb", same_core)

    arrived = exchange(query_sums(mine, swap_core(mine), sent(scale_query, query_embed)), "ha")
    query_1, copies = call(
        query_update_kernel,
        "query_update",
        (half(local, BOTH), half(n_ha, local, BOTH)),
        [VMEM] * 2,
    )(arrived, scale_query)

    slab = exchange(copies, "ha")
    own, send = host_sums(arrived, DIM, slots)
    pair = (own + swap_core(send).astype(jnp.float32)).astype(jnp.bfloat16)
    arrived = exchange(pair, "pb", same_core)

    own, send = host_sums(slab, BOTH, slots)
    host_1, chunks = call(
        host_update_kernel,
        "host_update",
        (half(BLOCK, BOTH), half(chips, 2 * BLOCK, BOTH)),
        [VMEM] * 4,
    )(arrived, scale_host, own, swap_core(send))
    arrived = exchange(chunks, "pb", same_core)
    host_2 = sent(scale_host, jnp.sum(arrived[:, BLOCK:].astype(jnp.float32), axis=0))

    arrived = exchange(query_sums(arrived, swap_core(arrived[:, :BLOCK])), "ha")
    query_2 = sent(scale_query, jnp.sum(arrived.astype(jnp.float32), axis=0))

    def mean(embed, one, two):
        zero = embed.astype(jnp.float32)[None]
        total = zero + split_views(one).astype(jnp.float32) + split_views(two).astype(jnp.float32)
        return (total / (LAYERS + 1)).astype(jnp.bfloat16)

    return (mean(query_embed, query_1, query_2), mean(host_embed, host_1, host_2))


def solution(mesh):
    in_specs = (
        P(("pb", "ha"), None),
        P(("pb", "ha"), None),
        P(("pb", "ha")),
        P(("pb", "ha")),
        P(("pb", "ha")),
        P(("pb", "ha")),
        P(("pb", "ha"), None, None),
        P(None, ("pb", "ha")),
        P(("pb", "ha")),
    )
    out_specs = (P(None, ("pb", "ha"), None), P(None, ("pb", "ha"), None))
    return jax.shard_map(
        per_device, mesh=mesh, in_specs=in_specs, out_specs=out_specs, check_vma=False
    )
```

```python
import jax
import jax.numpy as jnp
from jax import lax
from jax.experimental import pallas as pl
from jax.experimental.pallas import tpu as pltpu
from jax.sharding import PartitionSpec as P

DIM = 128
BLOCK = 128
CAP = 16
LAYERS = 2
BOTH = 2 * DIM

ANY = pl.BlockSpec(memory_space=pl.ANY)
SMEM = pl.BlockSpec(memory_space=pltpu.SMEM)
VMEM = pl.BlockSpec(memory_space=pltpu.VMEM)


def call(kernel, name, outs, ins, scratch=(), flops=0):
    return pl.pallas_call(
        kernel,
        out_shape=outs,
        in_specs=ins,
        out_specs=jax.tree.map(lambda _: VMEM, outs),
        scratch_shapes=scratch,
        cost_estimate=pl.CostEstimate(flops=flops, bytes_accessed=2**21, transcendentals=0),
        compiler_params=pltpu.CompilerParams(vmem_limit_bytes=24 * 2**20),
        name=name,
    )


def half(*shape):
    return jax.ShapeDtypeStruct(shape, jnp.bfloat16)


def single(*shape):
    return jax.ShapeDtypeStruct(shape, jnp.float32)


def add_views(acc_ref, block, keep_ref, s, prod):
    acc_ref[block, :, :DIM] += keep_ref[0, s] * prod[:, :DIM]
    acc_ref[block, :, DIM:] += keep_ref[1, s] * prod[:, -DIM:]


def host_kernel(
    rows_ref, slots_ref, keep_ref, w_ref, q_ref, after_ref, own_ref, send_ref, acc_ref
):
    del after_ref
    acc_ref[...] = jnp.zeros_like(acc_ref)
    owned = own_ref.shape[0]
    n = BLOCK // q_ref.shape[1]
    for s in range(CAP):
        q = q_ref[pl.ds(rows_ref[s] * n, n)].reshape(BLOCK, q_ref.shape[2])
        prod = lax.dot_general(
            w_ref[s], q, (((0,), (0,)), ((), ())), preferred_element_type=jnp.float32
        )
        add_views(acc_ref, slots_ref[s], keep_ref, s, prod)
    own_ref[...] = acc_ref[:owned]
    send_ref[...] = acc_ref[owned:].astype(jnp.bfloat16)


def query_kernel(
    rows_ref, slots_ref, keep_ref, w_ref, mine_ref, other_ref, after_ref, out_ref, acc_ref
):
    del after_ref
    acc_ref[...] = jnp.zeros_like(acc_ref)
    owned = mine_ref.shape[0]
    for s in range(CAP):
        slot = slots_ref[s]
        at = slot % owned
        host = jnp.where(slot < owned, mine_ref[at], other_ref[at])
        prod = jnp.dot(w_ref[s], host, preferred_element_type=jnp.float32)
        add_views(acc_ref, rows_ref[s], keep_ref, s, prod)
    out_ref[...] = acc_ref[...].astype(jnp.bfloat16).reshape(out_ref.shape)


def next_rows(scale_ref, total):
    now = (scale_ref[...] * total).astype(jnp.bfloat16)
    return now, (scale_ref[...] * now.astype(jnp.float32)).astype(jnp.bfloat16)


def update_kernel(in_ref, scale_ref, after_ref, now_ref, copies_ref):
    del after_ref
    now, sent = next_rows(scale_ref, jnp.sum(in_ref[...].astype(jnp.float32), axis=0))
    now_ref[...] = now
    copies_ref[...] = jnp.broadcast_to(sent[None], copies_ref.shape)


def spread_kernel(scale_ref, embed_ref, after_ref, out_ref):
    del after_ref
    sent = (scale_ref[...] * embed_ref[...].astype(jnp.float32)).astype(jnp.bfloat16)
    out_ref[...] = jnp.broadcast_to(sent[None], out_ref.shape)


def cast_kernel(total_ref, after_ref, *out_refs):
    del after_ref
    for index, out_ref in enumerate(out_refs, 1):
        out_ref[...] = total_ref[index].astype(jnp.bfloat16)


def exchange(blocks, axis, groups=None):
    return lax.all_to_all(blocks, axis, 0, 0, axis_index_groups=groups, tiled=True)


def reverse_bits(index, bits):
    return sum(((index >> b) & 1) << (bits - 1 - b) for b in range(bits))


def split_views(both):
    return jnp.stack([both[:, :DIM], both[:, DIM:]])


def per_device(
    query_embed,
    host_embed,
    query_degree,
    host_degree,
    tile_rows,
    tile_cols,
    tile_counts,
    keep_mask,
    live_tiles,
):
    n_pb, n_ha = lax.axis_size("pb"), lax.axis_size("ha")
    local = query_embed.shape[0]
    slab_blocks = n_ha * local // BLOCK
    chips = n_pb // 2
    core = lax.axis_index("pb") % 2
    same_core = [[2 * y + c for y in range(chips)] for c in range(2)]

    rows = tile_rows % slab_blocks
    cols = tile_cols // n_ha
    slots = ((cols % 2) ^ core) * chips + cols // 2
    bits = n_pb.bit_length() - 1
    by_bits = reverse_bits(cols ^ lax.axis_index("pb"), bits)
    live = jnp.arange(CAP, dtype=jnp.int32) < live_tiles[0]
    keep = (keep_mask * live[None]).astype(jnp.float32)
    weights = tile_counts.astype(jnp.bfloat16)
    scale_query = lax.rsqrt(query_degree.astype(jnp.float32))[:, None]
    scale_host = lax.rsqrt(host_degree.astype(jnp.float32))[:, None]

    def sent(scale, now):
        return (scale * now.astype(jnp.float32)).astype(jnp.bfloat16)

    def swap(blocks, axis, bit):
        size = lax.axis_size(axis)
        return lax.ppermute(blocks, axis, [(i, i ^ (1 << bit)) for i in range(size)])

    def swap_core(blocks):
        return swap(blocks, "pb", 0)

    def host_sums(slab, after):
        return call(
            host_kernel,
            "host_sums",
            (single(chips, BLOCK, BOTH), half(chips, BLOCK, BOTH)),
            [SMEM, SMEM, SMEM, VMEM, VMEM, ANY],
            [pltpu.VMEM((n_pb, BLOCK, BOTH), jnp.float32)],
            2 * CAP * BLOCK * BLOCK * slab.shape[2],
        )(rows, by_bits, keep, weights, slab, after)

    def query_sums(mine, slots, after):
        return call(
            query_kernel,
            "query_sums",
            half(n_ha, local, BOTH),
            [SMEM, SMEM, SMEM, VMEM, VMEM, VMEM, ANY],
            [pltpu.VMEM((slab_blocks, BLOCK, BOTH), jnp.float32)],
            2 * CAP * BLOCK * BLOCK * mine.shape[2],
        )(rows, slots, keep, weights, mine, swap_core(mine), after)

    def gather_steps(block):
        steps = [block[None]]
        for bit in range(bits - 1, 0, -1):
            steps.append(jnp.concatenate([steps[-1], swap(steps[-1], "pb", bit)]))
        return steps

    def reduce_steps(own, send):
        steps = [own + swap_core(send).astype(jnp.float32)]
        for bit in range(1, bits):
            total = steps[-1]
            size = total.shape[0] // 2
            other = swap(total[size:].astype(jnp.bfloat16), "pb", bit)
            steps.append(total[:size] + other.astype(jnp.float32))
        return steps

    def update(name, arrived, scale, copies, after):
        shape = arrived.shape[1:]
        return call(
            update_kernel, name, (half(*shape), half(copies, *shape)), [VMEM, VMEM, ANY]
        )(arrived, scale, after)

    def spread(name, scale, embed, copies, after):
        return call(spread_kernel, name, half(copies, *embed.shape), [VMEM, VMEM, ANY])(
            scale, embed, after
        )

    mine = exchange(spread("host_spread", scale_host, host_embed, chips, query_embed), "pb", same_core)
    slab = exchange(spread("query_spread", scale_query, query_embed, n_ha, mine), "ha")
    part = query_sums(mine, slots, mine)
    arrived = exchange(part, "ha")
    sums_0 = reduce_steps(*host_sums(slab, part))
    query_1, copies = update("query_update", arrived, scale_query, n_ha, sums_0[0])

    slab = exchange(copies, "ha")
    host_1, copies = update("host_update", sums_0[-1], scale_host, chips, slab)
    mine = exchange(copies, "pb", same_core)
    own, send = host_sums(slab, copies)
    total = own + swap_core(send).astype(jnp.float32)
    size = total.shape[0] // 2
    total = total[:size] + swap(total[size:].astype(jnp.bfloat16), "pb", 1).astype(jnp.float32)
    part = query_sums(mine, slots, mine)
    arrived = exchange(part, "ha")
    blocks = call(cast_kernel, "cast", (half(BLOCK, BOTH),) * (size - 1), [VMEM, ANY])(total, part)
    host_sum = total[0]
    for index, block in enumerate(blocks, 1):
        away = reverse_bits(index, bits - 2) << 2
        other = lax.ppermute(block, "pb", [(i, i ^ away) for i in range(n_pb)])
        host_sum = host_sum + other.astype(jnp.float32)
    host_2 = sent(scale_host, host_sum)
    query_2 = sent(scale_query, jnp.sum(arrived.astype(jnp.float32), axis=0))

    def mean(embed, one, two):
        zero = embed.astype(jnp.float32)[None]
        total = zero + split_views(one).astype(jnp.float32) + split_views(two).astype(jnp.float32)
        return (total / (LAYERS + 1)).astype(jnp.bfloat16)

    return (mean(query_embed, query_1, query_2), mean(host_embed, host_1, host_2))


def solution(mesh):
    in_specs = (
        P(("pb", "ha"), None),
        P(("pb", "ha"), None),
        P(("pb", "ha")),
        P(("pb", "ha")),
        P(("pb", "ha")),
        P(("pb", "ha")),
        P(("pb", "ha"), None, None),
        P(None, ("pb", "ha")),
        P(("pb", "ha")),
    )
    out_specs = (P(None, ("pb", "ha"), None), P(None, ("pb", "ha"), None))
    return jax.shard_map(
        per_device, mesh=mesh, in_specs=in_specs, out_specs=out_specs, check_vma=False
    )
```

```python
import jax
import jax.numpy as jnp
from jax import lax
from jax.experimental import pallas as pl
from jax.experimental.pallas import tpu as pltpu
from jax.sharding import PartitionSpec as P

DIM = 128
BLOCK = 128
CAP = 16
LAYERS = 2
BOTH = 2 * DIM

ANY = pl.BlockSpec(memory_space=pl.ANY)
SMEM = pl.BlockSpec(memory_space=pltpu.SMEM)
VMEM = pl.BlockSpec(memory_space=pltpu.VMEM)


def call(kernel, name, outs, ins, scratch=(), flops=0):
    return pl.pallas_call(
        kernel,
        out_shape=outs,
        in_specs=ins,
        out_specs=jax.tree.map(lambda _: VMEM, outs),
        scratch_shapes=scratch,
        cost_estimate=pl.CostEstimate(flops=flops, bytes_accessed=2**21, transcendentals=0),
        compiler_params=pltpu.CompilerParams(vmem_limit_bytes=24 * 2**20),
        name=name,
    )


def half(*shape):
    return jax.ShapeDtypeStruct(shape, jnp.bfloat16)


def single(*shape):
    return jax.ShapeDtypeStruct(shape, jnp.float32)


def add_views(acc_ref, block, keep_ref, s, prod):
    acc_ref[block, :, :DIM] += keep_ref[0, s] * prod[:, :DIM]
    acc_ref[block, :, DIM:] += keep_ref[1, s] * prod[:, -DIM:]


def host_kernel(
    rows_ref, slots_ref, keep_ref, w_ref, q_ref, after_ref, own_ref, send_ref, acc_ref
):
    del after_ref
    acc_ref[...] = jnp.zeros_like(acc_ref)
    owned = own_ref.shape[0]
    n = BLOCK // q_ref.shape[1]
    for s in range(CAP):
        q = q_ref[pl.ds(rows_ref[s] * n, n)].reshape(BLOCK, q_ref.shape[2])
        prod = lax.dot_general(
            w_ref[s], q, (((0,), (0,)), ((), ())), preferred_element_type=jnp.float32
        )
        add_views(acc_ref, slots_ref[s], keep_ref, s, prod)
    own_ref[...] = acc_ref[:owned]
    send_ref[...] = acc_ref[owned:].astype(jnp.bfloat16)


def query_kernel(
    rows_ref, slots_ref, keep_ref, w_ref, mine_ref, other_ref, after_ref, out_ref, acc_ref
):
    del after_ref
    acc_ref[...] = jnp.zeros_like(acc_ref)
    owned = mine_ref.shape[0]
    for s in range(CAP):
        slot = slots_ref[s]
        at = slot % owned
        host = jnp.where(slot < owned, mine_ref[at], other_ref[at])
        prod = jnp.dot(w_ref[s], host, preferred_element_type=jnp.float32)
        add_views(acc_ref, rows_ref[s], keep_ref, s, prod)
    out_ref[...] = acc_ref[...].astype(jnp.bfloat16).reshape(out_ref.shape)


def next_rows(scale_ref, total):
    now = (scale_ref[...] * total).astype(jnp.bfloat16)
    return now, (scale_ref[...] * now.astype(jnp.float32)).astype(jnp.bfloat16)


def update_kernel(in_ref, scale_ref, after_ref, now_ref, copies_ref):
    del after_ref
    now, sent = next_rows(scale_ref, jnp.sum(in_ref[...].astype(jnp.float32), axis=0))
    now_ref[...] = now
    copies_ref[...] = jnp.broadcast_to(sent[None], copies_ref.shape)


def spread_kernel(scale_ref, embed_ref, after_ref, out_ref):
    del after_ref
    sent = (scale_ref[...] * embed_ref[...].astype(jnp.float32)).astype(jnp.bfloat16)
    out_ref[...] = jnp.broadcast_to(sent[None], out_ref.shape)


def cast_kernel(total_ref, after_ref, *out_refs):
    del after_ref
    for index, out_ref in enumerate(out_refs, 1):
        out_ref[...] = total_ref[index].astype(jnp.bfloat16)


def exchange(blocks, axis, groups=None):
    return lax.all_to_all(blocks, axis, 0, 0, axis_index_groups=groups, tiled=True)


def place(index, order):
    return sum(((index >> b) & 1) << (len(order) - 1 - i) for i, b in enumerate(order))


def split_views(both):
    return jnp.stack([both[:, :DIM], both[:, DIM:]])


def per_device(
    query_embed,
    host_embed,
    query_degree,
    host_degree,
    tile_rows,
    tile_cols,
    tile_counts,
    keep_mask,
    live_tiles,
):
    n_pb, n_ha = lax.axis_size("pb"), lax.axis_size("ha")
    local = query_embed.shape[0]
    slab_blocks = n_ha * local // BLOCK
    chips = n_pb // 2
    core = lax.axis_index("pb") % 2
    same_core = [[2 * y + c for y in range(chips)] for c in range(2)]

    rows = tile_rows % slab_blocks
    cols = tile_cols // n_ha
    slots = ((cols % 2) ^ core) * chips + cols // 2
    halving_0, halving_1 = (0, 3, 1, 2), (0, 2, 1, 3)
    away = cols ^ lax.axis_index("pb")
    live = jnp.arange(CAP, dtype=jnp.int32) < live_tiles[0]
    keep = (keep_mask * live[None]).astype(jnp.float32)
    weights = tile_counts.astype(jnp.bfloat16)
    scale_query = lax.rsqrt(query_degree.astype(jnp.float32))[:, None]
    scale_host = lax.rsqrt(host_degree.astype(jnp.float32))[:, None]

    def sent(scale, now):
        return (scale * now.astype(jnp.float32)).astype(jnp.bfloat16)

    def swap(blocks, axis, bit):
        size = lax.axis_size(axis)
        return lax.ppermute(blocks, axis, [(i, i ^ (1 << bit)) for i in range(size)])

    def swap_core(blocks):
        return swap(blocks, "pb", 0)

    def host_sums(slab, halving, after):
        return call(
            host_kernel,
            "host_sums",
            (single(chips, BLOCK, BOTH), half(chips, BLOCK, BOTH)),
            [SMEM, SMEM, SMEM, VMEM, VMEM, ANY],
            [pltpu.VMEM((n_pb, BLOCK, BOTH), jnp.float32)],
            2 * CAP * BLOCK * BLOCK * slab.shape[2],
        )(rows, place(away, halving), keep, weights, slab, after)

    def query_sums(mine, slots, after):
        return call(
            query_kernel,
            "query_sums",
            half(n_ha, local, BOTH),
            [SMEM, SMEM, SMEM, VMEM, VMEM, VMEM, ANY],
            [pltpu.VMEM((slab_blocks, BLOCK, BOTH), jnp.float32)],
            2 * CAP * BLOCK * BLOCK * mine.shape[2],
        )(rows, slots, keep, weights, mine, swap_core(mine), after)

    def halve(total, bit):
        size = total.shape[0] // 2
        return total[:size] + swap(total[size:].astype(jnp.bfloat16), "pb", bit).astype(jnp.float32)

    def update(name, arrived, scale, copies, after):
        shape = arrived.shape[1:]
        return call(
            update_kernel, name, (half(*shape), half(copies, *shape)), [VMEM, VMEM, ANY]
        )(arrived, scale, after)

    def spread(name, scale, embed, copies, after):
        return call(spread_kernel, name, half(copies, *embed.shape), [VMEM, VMEM, ANY])(
            scale, embed, after
        )

    mine = exchange(spread("host_spread", scale_host, host_embed, chips, query_embed), "pb", same_core)
    slab = exchange(spread("query_spread", scale_query, query_embed, n_ha, mine), "ha")
    part = query_sums(mine, slots, mine)
    arrived = exchange(part, "ha")
    own, send = host_sums(slab, halving_0, part)
    cores = own + swap_core(send).astype(jnp.float32)
    total = cores
    for bit in halving_0[1:]:
        total = halve(total, bit)
    query_1, copies = update("query_update", arrived, scale_query, n_ha, cores)

    slab = exchange(copies, "ha")
    host_1, copies = update("host_update", total, scale_host, chips, slab)
    mine = exchange(copies, "pb", same_core)
    own, send = host_sums(slab, halving_1, copies)
    total = halve(own + swap_core(send).astype(jnp.float32), halving_1[1])
    part = query_sums(mine, slots, mine)
    arrived = exchange(part, "ha")
    blocks = (half(BLOCK, BOTH),) * (total.shape[0] - 1)
    blocks = call(cast_kernel, "cast", blocks, [VMEM, ANY])(total, part)
    host_sum = total[0]
    for index, block in enumerate(blocks, 1):
        across = ((index >> 1) << halving_1[2]) | ((index & 1) << halving_1[3])
        other = lax.ppermute(block, "pb", [(i, i ^ across) for i in range(n_pb)])
        host_sum = host_sum + other.astype(jnp.float32)
    host_2 = sent(scale_host, host_sum)
    query_2 = sent(scale_query, jnp.sum(arrived.astype(jnp.float32), axis=0))

    def mean(embed, one, two):
        zero = embed.astype(jnp.float32)[None]
        total = zero + split_views(one).astype(jnp.float32) + split_views(two).astype(jnp.float32)
        return (total / (LAYERS + 1)).astype(jnp.bfloat16)

    return (mean(query_embed, query_1, query_2), mean(host_embed, host_1, host_2))


def solution(mesh):
    in_specs = (
        P(("pb", "ha"), None),
        P(("pb", "ha"), None),
        P(("pb", "ha")),
        P(("pb", "ha")),
        P(("pb", "ha")),
        P(("pb", "ha")),
        P(("pb", "ha"), None, None),
        P(None, ("pb", "ha")),
        P(("pb", "ha")),
    )
    out_specs = (P(None, ("pb", "ha"), None), P(None, ("pb", "ha"), None))
    return jax.shard_map(
        per_device, mesh=mesh, in_specs=in_specs, out_specs=out_specs, check_vma=False
    )
```

```python
import jax
import jax.numpy as jnp
from jax import lax
from jax.experimental import pallas as pl
from jax.experimental.pallas import tpu as pltpu
from jax.sharding import PartitionSpec as P

DIM = 128
BLOCK = 128
CAP = 16
LAYERS = 2
BOTH = 2 * DIM

ANY = pl.BlockSpec(memory_space=pl.ANY)
SMEM = pl.BlockSpec(memory_space=pltpu.SMEM)
VMEM = pl.BlockSpec(memory_space=pltpu.VMEM)


def call(kernel, name, outs, ins, scratch=(), flops=0):
    return pl.pallas_call(
        kernel,
        out_shape=outs,
        in_specs=ins,
        out_specs=jax.tree.map(lambda _: VMEM, outs),
        scratch_shapes=scratch,
        cost_estimate=pl.CostEstimate(flops=flops, bytes_accessed=2**21, transcendentals=0),
        compiler_params=pltpu.CompilerParams(vmem_limit_bytes=24 * 2**20),
        name=name,
    )


def half(*shape):
    return jax.ShapeDtypeStruct(shape, jnp.bfloat16)


def single(*shape):
    return jax.ShapeDtypeStruct(shape, jnp.float32)


def add_views(acc_ref, block, keep_ref, s, prod):
    acc_ref[block, :, :DIM] += keep_ref[0, s] * prod[:, :DIM]
    acc_ref[block, :, DIM:] += keep_ref[1, s] * prod[:, -DIM:]


def host_kernel(
    rows_ref, slots_ref, keep_ref, w_ref, q_ref, after_ref, own_ref, send_ref, acc_ref
):
    del after_ref
    acc_ref[...] = jnp.zeros_like(acc_ref)
    owned = own_ref.shape[0]
    n = BLOCK // q_ref.shape[1]
    for s in range(CAP):
        q = q_ref[pl.ds(rows_ref[s] * n, n)].reshape(BLOCK, q_ref.shape[2])
        prod = lax.dot_general(
            w_ref[s], q, (((0,), (0,)), ((), ())), preferred_element_type=jnp.float32
        )
        add_views(acc_ref, slots_ref[s], keep_ref, s, prod)
    own_ref[...] = acc_ref[:owned]
    send_ref[...] = acc_ref[owned:].astype(jnp.bfloat16)


def query_kernel(
    rows_ref, slots_ref, keep_ref, w_ref, mine_ref, other_ref, after_ref, out_ref, acc_ref
):
    del after_ref
    acc_ref[...] = jnp.zeros_like(acc_ref)
    owned = mine_ref.shape[0]
    for s in range(CAP):
        slot = slots_ref[s]
        at = slot % owned
        host = jnp.where(slot < owned, mine_ref[at], other_ref[at])
        prod = jnp.dot(w_ref[s], host, preferred_element_type=jnp.float32)
        add_views(acc_ref, rows_ref[s], keep_ref, s, prod)
    out_ref[...] = acc_ref[...].astype(jnp.bfloat16).reshape(out_ref.shape)


def next_rows(scale_ref, total):
    now = (scale_ref[...] * total).astype(jnp.bfloat16)
    return now, (scale_ref[...] * now.astype(jnp.float32)).astype(jnp.bfloat16)


def update_kernel(in_ref, scale_ref, after_ref, now_ref, copies_ref):
    del after_ref
    now, sent = next_rows(scale_ref, jnp.sum(in_ref[...].astype(jnp.float32), axis=0))
    now_ref[...] = now
    copies_ref[...] = jnp.broadcast_to(sent[None], copies_ref.shape)


def spread_kernel(scale_ref, embed_ref, after_ref, out_ref):
    del after_ref
    sent = (scale_ref[...] * embed_ref[...].astype(jnp.float32)).astype(jnp.bfloat16)
    out_ref[...] = jnp.broadcast_to(sent[None], out_ref.shape)


def cast_kernel(total_ref, after_ref, *out_refs):
    del after_ref
    for index, out_ref in enumerate(out_refs, 1):
        out_ref[...] = total_ref[index].astype(jnp.bfloat16)


def exchange(blocks, axis, groups=None):
    return lax.all_to_all(blocks, axis, 0, 0, axis_index_groups=groups, tiled=True)


def place(index, order):
    return sum(((index >> b) & 1) << (len(order) - 1 - i) for i, b in enumerate(order))


def split_views(both):
    return jnp.stack([both[:, :DIM], both[:, DIM:]])


def per_device(
    query_embed,
    host_embed,
    query_degree,
    host_degree,
    tile_rows,
    tile_cols,
    tile_counts,
    keep_mask,
    live_tiles,
):
    n_pb, n_ha = lax.axis_size("pb"), lax.axis_size("ha")
    local = query_embed.shape[0]
    slab_blocks = n_ha * local // BLOCK
    chips = n_pb // 2
    core = lax.axis_index("pb") % 2
    same_core = [[2 * y + c for y in range(chips)] for c in range(2)]

    rows = tile_rows % slab_blocks
    cols = tile_cols // n_ha
    slots = ((cols % 2) ^ core) * chips + cols // 2
    halving_0, halving_1 = (0, 3, 1, 2), (0, 1, 3, 2)
    away = cols ^ lax.axis_index("pb")
    live = jnp.arange(CAP, dtype=jnp.int32) < live_tiles[0]
    keep = (keep_mask * live[None]).astype(jnp.float32)
    weights = tile_counts.astype(jnp.bfloat16)
    scale_query = lax.rsqrt(query_degree.astype(jnp.float32))[:, None]
    scale_host = lax.rsqrt(host_degree.astype(jnp.float32))[:, None]

    def sent(scale, now):
        return (scale * now.astype(jnp.float32)).astype(jnp.bfloat16)

    def swap(blocks, axis, bit):
        size = lax.axis_size(axis)
        return lax.ppermute(blocks, axis, [(i, i ^ (1 << bit)) for i in range(size)])

    def swap_core(blocks):
        return swap(blocks, "pb", 0)

    def host_sums(slab, halving, after):
        return call(
            host_kernel,
            "host_sums",
            (single(chips, BLOCK, BOTH), half(chips, BLOCK, BOTH)),
            [SMEM, SMEM, SMEM, VMEM, VMEM, ANY],
            [pltpu.VMEM((n_pb, BLOCK, BOTH), jnp.float32)],
            2 * CAP * BLOCK * BLOCK * slab.shape[2],
        )(rows, place(away, halving), keep, weights, slab, after)

    def query_sums(mine, slots, after):
        return call(
            query_kernel,
            "query_sums",
            half(n_ha, local, BOTH),
            [SMEM, SMEM, SMEM, VMEM, VMEM, VMEM, ANY],
            [pltpu.VMEM((slab_blocks, BLOCK, BOTH), jnp.float32)],
            2 * CAP * BLOCK * BLOCK * mine.shape[2],
        )(rows, slots, keep, weights, mine, swap_core(mine), after)

    def halve(total, bit):
        size = total.shape[0] // 2
        return total[:size] + swap(total[size:].astype(jnp.bfloat16), "pb", bit).astype(jnp.float32)

    def update(name, arrived, scale, copies, after):
        shape = arrived.shape[1:]
        return call(
            update_kernel, name, (half(*shape), half(copies, *shape)), [VMEM, VMEM, ANY]
        )(arrived, scale, after)

    def spread(name, scale, embed, copies, after):
        return call(spread_kernel, name, half(copies, *embed.shape), [VMEM, VMEM, ANY])(
            scale, embed, after
        )

    mine = exchange(spread("host_spread", scale_host, host_embed, chips, query_embed), "pb", same_core)
    slab = exchange(spread("query_spread", scale_query, query_embed, n_ha, mine), "ha")
    part = query_sums(mine, slots, mine)
    arrived = exchange(part, "ha")
    own, send = host_sums(slab, halving_0, part)
    cores = own + swap_core(send).astype(jnp.float32)
    total = cores
    for bit in halving_0[1:]:
        total = halve(total, bit)
    query_1, copies = update("query_update", arrived, scale_query, n_ha, cores)

    slab = exchange(copies, "ha")
    host_1, copies = update("host_update", total, scale_host, chips, slab)
    mine = exchange(copies, "pb", same_core)
    own, send = host_sums(slab, halving_1, copies)
    total = halve(own + swap_core(send).astype(jnp.float32), halving_1[1])
    part = query_sums(mine, slots, mine)
    arrived = exchange(part, "ha")
    blocks = (half(BLOCK, BOTH),) * (total.shape[0] - 1)
    blocks = call(cast_kernel, "cast", blocks, [VMEM, ANY])(total, part)
    host_sum = total[0]
    for index, block in enumerate(blocks, 1):
        across = ((index >> 1) << halving_1[2]) | ((index & 1) << halving_1[3])
        other = lax.ppermute(block, "pb", [(i, i ^ across) for i in range(n_pb)])
        host_sum = host_sum + other.astype(jnp.float32)
    host_2 = sent(scale_host, host_sum)
    query_2 = sent(scale_query, jnp.sum(arrived.astype(jnp.float32), axis=0))

    def mean(embed, one, two):
        zero = embed.astype(jnp.float32)[None]
        total = zero + split_views(one).astype(jnp.float32) + split_views(two).astype(jnp.float32)
        return (total / (LAYERS + 1)).astype(jnp.bfloat16)

    return (mean(query_embed, query_1, query_2), mean(host_embed, host_1, host_2))


def solution(mesh):
    in_specs = (
        P(("pb", "ha"), None),
        P(("pb", "ha"), None),
        P(("pb", "ha")),
        P(("pb", "ha")),
        P(("pb", "ha")),
        P(("pb", "ha")),
        P(("pb", "ha"), None, None),
        P(None, ("pb", "ha")),
        P(("pb", "ha")),
    )
    out_specs = (P(None, ("pb", "ha"), None), P(None, ("pb", "ha"), None))
    return jax.shard_map(
        per_device, mesh=mesh, in_specs=in_specs, out_specs=out_specs, check_vma=False
    )
```
